256 devices in a mesh: imp: 64 (over y, z, core), ad: 4 (over x).
Axes of the slice: x: 4, y: 4, z: 8, core: 2. Of those that a mesh axis runs over, the one named last changes fastest.
Arguments:
- imp_vectors: bfloat16 [65536, 128], P('imp'), may hold values from -32 to 32
- ad_vectors: bfloat16 [1572864, 128], P(('imp', 'ad')), may hold values from -1 to 1
- spend_limits: float32 [1572864], P(('imp', 'ad')), may hold values from 0.005 to 0.05
- targets: int32 [64, 4, 32], P('imp', 'ad'), may hold values from 0 to 3071, as said below
Outputs:
- pacing: float32 [1572864], P(('imp', 'ad'))
- prices: float32 [65536], P('imp')
The draws below stay inside these ranges and needn't reach their ends.
Inputs may be any that keep to these rules, and one draw needn't show every extreme that they name: No block appears twice in one list targets[i, a, :]; at most 2 entries of one list share the owner q // 48, and in each column a some owner gets exactly 2 entries from every impression block.
All inputs are finite; a program needn't handle non-finite values.
Results may differ from the reference program's by a relative error of at most 0.0003.
Values may be sent and summed in bfloat16 or wider, within the bound.
No kernel may reach another device: no remote copies, remote signals or barrier semaphores. Data moves between devices by JAX's collectives and lax.ppermute only.
A program may use at most 128 MiB of HBM per device.

```python
import math
import jax
import jax.numpy as jnp
from jax import lax

EMB = 128
BLOCK = 128
IMP_DEV = 1024
K_DEV = 32
ABLK_DEV = 48
ROUNDS = 4
IMP_BLOCKS = 64
AD_SHARDS = 4
CAP = 2
IMPRESSIONS = 65536
ADS = 1572864


def draw_imp_vectors(key, part):
    key = jax.random.fold_in(key, 3)
    rows = jax.random.normal(key, (IMPRESSIONS, EMB), jnp.float32)
    return jnp.clip(rows, -4.0, 4.0).astype(jnp.bfloat16)


def draw_ad_vectors(key, part):
    key = jax.random.fold_in(key, 5)
    noise = jax.random.normal(key, (ADS, EMB), jnp.float32) * EMB ** (-0.5)
    return jnp.clip(noise, -1.0, 1.0).astype(jnp.bfloat16)


def draw_targets(key, part):
    key = jax.random.fold_in(key, 7)
    owner_total = IMP_BLOCKS
    hot_owner = jax.random.randint(jax.random.fold_in(key, 1), (AD_SHARDS,), 0, owner_total)
    base_key = jax.random.fold_in(key, 4)

    def one_list(list_index, hot):
        device_key = jax.random.fold_in(base_key, list_index)
        others = jax.random.permutation(jax.random.fold_in(device_key, 2), owner_total - 1)
        others = others + (others >= hot).astype(jnp.int32)
        slot_order = jnp.arange(K_DEV, dtype=jnp.int32)
        rest = slot_order - CAP
        pick = jnp.where(slot_order < CAP, 0, rest % (owner_total - 1))
        owner_of = jnp.where(slot_order < CAP, hot, others[pick])
        rank_of = jnp.where(slot_order < CAP, slot_order, rest // (owner_total - 1))
        offset = jax.random.randint(jax.random.fold_in(device_key, 3), (owner_total,), 0, ABLK_DEV)
        local_of = (offset[owner_of] + rank_of) % ABLK_DEV
        return (owner_of * ABLK_DEV + local_of).astype(jnp.int32)
    list_index = jnp.arange(IMP_BLOCKS, dtype=jnp.int32)[:, None] * AD_SHARDS + jnp.arange(AD_SHARDS, dtype=jnp.int32)[None, :]
    per_column = jax.vmap(one_list, in_axes=(0, 0))
    return jax.vmap(per_column, in_axes=(0, None))(list_index, hot_owner)


def shard_levels(stream_key, dims, split, least, high):
    def one(axis_at, parts):
        draws = jax.random.uniform(jax.random.fold_in(jax.random.fold_in(stream_key, 6), axis_at), (parts,), jnp.float32, least / len(split), high / len(split))
        return jnp.repeat(jnp.exp(draws), dims[axis_at] // parts).reshape((-1,) + (1,) * (len(dims) - axis_at - 1))

    level = one(*split[0])
    for cut in split[1:]:
        level = level * one(*cut)
    return level


def setup_inputs(seed: int = 0) -> dict:
    key_of = jax.random.split(jax.random.key(seed), 5)
    imp_vectors = draw_imp_vectors(jax.random.fold_in(key_of[4], 71), 0)
    ad_vectors = draw_ad_vectors(jax.random.fold_in(key_of[4], 71), 0)
    spend_limits = jnp.clip(jnp.exp(math.log(0.05) - 2.3025851 * jax.random.uniform(key_of[2], (ADS,), jnp.float32) ** shard_levels(key_of[2], (ADS,), ((0, 256),), -0.2, 0.2)), 0.005, 0.05)
    targets = draw_targets(jax.random.fold_in(key_of[4], 71), 0)
    return dict(imp_vectors=imp_vectors, ad_vectors=ad_vectors, spend_limits=spend_limits, targets=targets)


softness_level = 0.5
util_floor = 0.01
pacing_cap = 3.0

def reference(imp_vectors, ad_vectors, spend_limits, targets):
    block_total = ADS // BLOCK
    vectors = ad_vectors.reshape(block_total, BLOCK, EMB)
    column = jnp.arange(AD_SHARDS, dtype=jnp.int32)
    owner_of = targets // ABLK_DEV
    local_of = targets % ABLK_DEV
    block_ids = ((owner_of * AD_SHARDS + column[None, :, None]) * ABLK_DEV + local_of).astype(jnp.int32)
    imp_blocks = imp_vectors.reshape(IMP_BLOCKS, IMP_DEV, EMB)
    limit_rows = spend_limits.reshape(block_total, BLOCK)
    pacing = jnp.ones((block_total, BLOCK), jnp.float32)
    prices = jnp.zeros((IMP_BLOCKS, IMP_DEV), jnp.float32)
    for step in range(ROUNDS):

        def per_block(bidder_utility, inputs):
            imp_rows, ids = inputs
            flattened_indices = ids.reshape(-1).astype(jnp.int32)
            chosen = vectors[flattened_indices].reshape(-1, EMB)
            value_matrix = jax.nn.softplus(jnp.dot(imp_rows, chosen.T, preferred_element_type=jnp.float32))
            scaled_scores = value_matrix * pacing[flattened_indices].reshape(-1)[None, :] / softness_level
            top = lax.optimization_barrier(jnp.max(scaled_scores, axis=1, keepdims=True))
            log_sum_exponent = top + jnp.log(lax.optimization_barrier(jnp.sum(jnp.exp(scaled_scores - top), axis=1, keepdims=True)))
            share = jnp.exp(scaled_scores - log_sum_exponent)
            terms = lax.optimization_barrier(jnp.sum(share * value_matrix, axis=0)).reshape(-1, BLOCK)
            bidder_utility = bidder_utility.at[flattened_indices].add(terms)
            return (bidder_utility, softness_level * log_sum_exponent[:, 0])
        bidder_utility, prices = lax.scan(per_block, jnp.zeros((block_total, BLOCK), jnp.float32), (imp_blocks, block_ids))
        target = jnp.minimum(limit_rows / jnp.maximum(bidder_utility, util_floor), pacing_cap)
        pacing = jnp.sqrt(pacing * target)
    return (pacing.reshape(-1), prices.reshape(-1))
```

```python
import functools
import math

import jax
import jax.numpy as jnp
from jax import lax
from jax.experimental import pallas as pl
from jax.experimental.pallas import tpu as pltpu
from jax.sharding import PartitionSpec as P

BLOCK = 128
ROUNDS = 4
CAP = 2
SHARED = 6
SLOTS = SHARED + CAP

softness_level = 0.5
util_floor = 0.01
pacing_cap = 3.0

LOG2E = math.log2(math.e)
LN2 = math.log(2.0)
SCALE = LOG2E / softness_level
HI = lax.Precision.HIGHEST
f32 = jnp.float32
bf16 = jnp.bfloat16
VMEM = pl.BlockSpec(memory_space=pltpu.VMEM)


def params(mib):
    return pltpu.CompilerParams(vmem_limit_bytes=mib * 2**20)


def pinned(x):
    return pltpu.with_memory_space_constraint(x, pltpu.VMEM)


def tn(a, b):
    return lax.dot_general(a, b, (((0,), (0,)), ((), ())), precision=HI, preferred_element_type=f32)


def nn(a, b):
    return lax.dot_general(a, b, (((1,), (0,)), ((), ())), precision=HI, preferred_element_type=f32)


def eye():
    return lax.broadcasted_iota(jnp.int32, (128, 128), 0) == lax.broadcasted_iota(
        jnp.int32, (128, 128), 1
    )


def values_kernel(blocks, x_ref, y_ref, v_ref, ya, yb, yt):
    parts = y_ref.shape[0] // blocks
    ya[...] = y_ref[:, :128].astype(f32)
    yb[...] = y_ref[:, 128:].astype(f32)

    def unpack(k, _):
        at = pl.multiple_of(k * BLOCK, BLOCK)
        yt[pl.ds(at, parts), :] = ya[pl.ds(k, parts, stride=blocks), :].astype(bf16)
        yt[pl.ds(at + parts, parts), :] = yb[pl.ds(k, parts, stride=blocks), :].astype(bf16)
        return 0

    lax.fori_loop(0, blocks, unpack, 0)
    tile_r, tile_c = 256, 512
    across = v_ref.shape[1] // tile_c

    def tile(step, _):
        rows = pl.ds(pl.multiple_of((step // across) * tile_r, tile_r), tile_r)
        cols = pl.ds(pl.multiple_of((step % across) * tile_c, tile_c), tile_c)
        s = lax.dot_general(
            x_ref[rows, :], yt[cols, :], (((1,), (1,)), ((), ())), preferred_element_type=f32
        )
        v_ref[rows, cols] = jnp.maximum(s, 0.0) + LN2 * jnp.log2(1.0 + jnp.exp2(jnp.abs(s) * -LOG2E))
        return 0

    lax.fori_loop(0, (v_ref.shape[0] // tile_r) * across, tile, 0)


def values_call(x, y, blocks):
    rows, width = x.shape[0], blocks * BLOCK
    return pl.pallas_call(
        functools.partial(values_kernel, blocks),
        out_shape=pltpu.VMEM((rows, width), f32),
        in_specs=[VMEM, VMEM],
        out_specs=VMEM,
        scratch_shapes=[
            pltpu.VMEM((y.shape[0], 128), f32),
            pltpu.VMEM((y.shape[0], 128), f32),
            pltpu.VMEM((width, 128), bf16),
        ],
        compiler_params=params(16),
    )(x, y)


def score(v_ref, ev_ref, ms_ref, pace, mcol, scol):
    rows, width = v_ref.shape
    step_rows = 32

    def body(step, _):
        for part in range(step_rows // 8):
            at = pl.ds(pl.multiple_of(step * step_rows, step_rows) + part * 8, 8)
            v = v_ref[at, :]
            t = v * pace[...]
            m = jnp.max(t, axis=1, keepdims=True)
            e = jnp.exp2(t - m)
            ev_ref[at, :] = e * v
            mcol[at, :] = jnp.broadcast_to(m, (8, 128))
            scol[at, :] = jnp.broadcast_to(jnp.sum(e, axis=1, keepdims=True), (8, 128))
        return 0

    lax.fori_loop(0, rows // step_rows, body, 0)
    diagonal = eye()
    chunks = rows // 128
    for c in range(chunks):
        part = pl.ds(c * 128, 128)
        ms_ref[c : c + 1, :] = jnp.sum(jnp.where(diagonal, mcol[part, :], 0.0), axis=0, keepdims=True)
        ms_ref[chunks + c : chunks + c + 1, :] = jnp.sum(
            jnp.where(diagonal, scol[part, :], 0.0), axis=0, keepdims=True
        )


def first_score_kernel(flag_ref, v_ref, ev_ref, ms_ref, pace, mcol, scol):
    pace[...] = jnp.full(pace.shape, SCALE, f32)
    ms_ref[16:24, :] = flag_ref[...]
    score(v_ref, ev_ref, ms_ref, pace, mcol, scol)


def pace_step(pace, util, limit):
    return jnp.sqrt(pace * jnp.minimum(limit / jnp.maximum(util, util_floor), pacing_cap))


def spread_pace(p, pace):
    for k in range(p.shape[0]):
        pace[:, k * BLOCK : (k + 1) * BLOCK] = jnp.broadcast_to(p[k : k + 1, :] * SCALE, (8, BLOCK))


def second_score_kernel(
    util_ref, recv_ref, pick_ref, extra_ref, v_ref, ev_ref, ms_ref, p_ref, limit_ref, pace, mcol, scol
):
    blocks = util_ref.shape[0]
    got = tn(pick_ref[...], recv_ref[...])
    util = util_ref[...] + extra_ref[...] + got[:blocks, :]
    limit = got[blocks:, :]
    p = pace_step(jnp.ones(util.shape, f32), util, limit)
    p_ref[...] = p
    limit_ref[...] = limit
    spread_pace(p, pace)
    score(v_ref, ev_ref, ms_ref, pace, mcol, scol)


def score_kernel(
    util_ref, recv_ref, pick_ref, extra_ref, limit_ref, old_ref, v_ref, ev_ref, ms_ref, p_ref, pace, mcol, scol
):
    util = util_ref[...] + extra_ref[...] + tn(pick_ref[...], recv_ref[...])
    p = pace_step(old_ref[...], util, limit_ref[...])
    p_ref[...] = p
    spread_pace(p, pace)
    score(v_ref, ev_ref, ms_ref, pace, mcol, scol)


def score_call(kernel, v, args, ms_rows, outs):
    rows, width = v.shape
    small = jax.ShapeDtypeStruct((width // BLOCK, BLOCK), f32)
    return pl.pallas_call(
        kernel,
        out_shape=[pltpu.VMEM((rows, width), f32), jax.ShapeDtypeStruct((ms_rows, 128), f32)] + [small] * outs,
        in_specs=[VMEM] * (len(args) + 1),
        out_specs=[VMEM] * (2 + outs),
        scratch_shapes=[
            pltpu.VMEM((8, width), f32),
            pltpu.VMEM((rows, 128), f32),
            pltpu.VMEM((rows, 128), f32),
        ],
        compiler_params=params(16),
    )(*args, pinned(v))


def combine(ms_ref, all_ref, chunks):
    tops = all_ref[:, 0:chunks, :]
    sums = all_ref[:, chunks : 2 * chunks, :]
    top = jnp.max(tops, axis=0)
    total = jnp.sum(sums * jnp.exp2(tops - top[None]), axis=0)
    lse = top + jnp.log2(total)
    return lse, jnp.exp2(ms_ref[0:chunks, :] - lse)


def utility(weight, ev_ref, util_ref, wcol):
    rows, width = ev_ref.shape
    diagonal = eye()
    for c in range(rows // 128):
        spread = jnp.where(diagonal, jnp.broadcast_to(weight[c : c + 1, :], (128, 128)), 0.0)
        wcol[c * 128 : (c + 1) * 128, :] = jnp.broadcast_to(
            jnp.sum(spread, axis=1, keepdims=True), (128, 128)
        )
    blocks = width // BLOCK

    def body(step, acc):
        out = list(acc)
        for part in range(2):
            at = pl.ds(pl.multiple_of(step * 16, 16) + part * 8, 8)
            w = wcol[at, :]
            for k in range(blocks):
                out[k] = out[k] + ev_ref[at, k * BLOCK : (k + 1) * BLOCK] * w
        return tuple(out)

    acc = lax.fori_loop(0, rows // 16, body, tuple(jnp.zeros((8, BLOCK), f32) for _ in range(blocks)))
    for k in range(blocks):
        util_ref[k : k + 1, :] = jnp.sum(acc[k], axis=0, keepdims=True)


def first_utility_kernel(ms_ref, all_ref, put_ref, own_put_ref, limit_ref, ev_ref, util_ref, send_ref, wcol):
    _, weight = combine(ms_ref, all_ref, ev_ref.shape[0] // 128)
    utility(weight, ev_ref, util_ref, wcol)
    send_ref[...] = nn(put_ref[...], util_ref[...]) + nn(own_put_ref[...], limit_ref[...])


def utility_kernel(ms_ref, all_ref, put_ref, ev_ref, util_ref, send_ref, wcol):
    _, weight = combine(ms_ref, all_ref, ev_ref.shape[0] // 128)
    utility(weight, ev_ref, util_ref, wcol)
    send_ref[...] = nn(put_ref[...], util_ref[...])


def last_utility_kernel(ms_ref, all_ref, put_ref, p_ref, ev_ref, util_ref, send_ref, price_ref, wcol):
    lse, weight = combine(ms_ref, all_ref, ev_ref.shape[0] // 128)
    price_ref[...] = lse * (softness_level * LN2)
    utility(weight, ev_ref, util_ref, wcol)
    send_ref[:, :BLOCK] = nn(put_ref[...], util_ref[...])
    send_ref[:, BLOCK:] = nn(put_ref[...], p_ref[...])


def utility_call(kernel, ev, args, send_shape, price):
    rows, width = ev.shape
    outs = [
        jax.ShapeDtypeStruct((width // BLOCK, BLOCK), f32),
        jax.ShapeDtypeStruct(send_shape, f32),
    ]
    if price:
        outs.append(jax.ShapeDtypeStruct((rows // 128, 128), f32))
    return pl.pallas_call(
        kernel,
        out_shape=outs,
        in_specs=[VMEM] * (len(args) + 1),
        out_specs=[VMEM] * len(outs),
        scratch_shapes=[pltpu.VMEM((rows, 128), f32)],
        compiler_params=params(16),
    )(*args, pinned(ev))


def last_pace_kernel(recv_ref, back_ref, limit_ref, out_ref):
    back = back_ref[...]
    limit = limit_ref[...]
    got = nn(back, recv_ref[...])
    count = jnp.sum(back, axis=1, keepdims=True)
    lone = jnp.ones(limit.shape, f32)
    for _ in range(ROUNDS - 1):
        lone = pace_step(lone, jnp.zeros(limit.shape, f32), limit)
    pace = jnp.where(count > 0.0, got[:, BLOCK:] / jnp.maximum(count, 1.0), lone)
    out_ref[...] = pace_step(pace, got[:, :BLOCK], limit)


def before(flags, axis):
    size = flags.shape[axis]
    order = jnp.arange(size)
    less = (order[:, None] < order[None, :]).astype(f32)
    moved = jnp.moveaxis(flags, axis, -1).astype(f32)
    return jnp.moveaxis(jnp.dot(moved, less), -1, axis).astype(jnp.int32)


def swap(x, axis):
    return lax.all_to_all(x, axis, split_axis=0, concat_axis=0, tiled=True)


def per_device(imp_vectors, ad_vectors, spend_limits, targets):
    owners = lax.axis_size("imp")
    columns = lax.axis_size("ad")
    me = lax.axis_index("imp")
    emb = imp_vectors.shape[1]
    own_blocks = ad_vectors.shape[0] // BLOCK
    wanted = targets.reshape(-1)
    size = wanted.shape[0]
    half = BLOCK // 2
    limits = spend_limits.reshape(own_blocks, BLOCK)

    lists = swap(jnp.broadcast_to(wanted[None, :], (owners, size)), "imp")
    pieces = ad_vectors.reshape(own_blocks, 2, half, emb).transpose(2, 0, 1, 3)
    table = swap(pieces.reshape(half, own_blocks, 2 * emb), "imp").reshape(owners * own_blocks, 2 * emb)
    chosen = table[lists.reshape(-1)].reshape(owners, size, 2 * emb)
    mine = swap(chosen, "imp").reshape(owners * size, 2 * emb)

    peer = jnp.arange(owners, dtype=jnp.int32)
    equal = (lists[:, :, None] == wanted[None, None, :]) & (peer != me)[:, None, None]
    gives = jnp.any(equal, axis=1)
    takes = jnp.any(equal, axis=2)
    slot = jnp.arange(SLOTS, dtype=jnp.int32)
    give_at = before(gives, 1)
    take_at = before(takes, 1)
    usable = (slot < SHARED)[None, :, None]
    put = ((give_at[:, None, :] == slot[None, :, None]) & gives[:, None, :] & usable).astype(f32)
    take_slot = ((take_at[:, None, :] == slot[None, :, None]) & takes[:, None, :] & usable).astype(f32)
    pick = jnp.einsum("isk,ikw->isw", take_slot, equal.astype(f32))
    put = put.reshape(owners * SLOTS, size)
    pick = pick.reshape(owners * SLOTS, size)
    holds = jnp.any(
        lists[:, :, None] == jnp.arange(owners * own_blocks, dtype=jnp.int32)[None, None, :], axis=1
    ).astype(bf16)
    common = lax.dot_general(holds, holds, (((1,), (1,)), ((), ())), preferred_element_type=f32)
    crowded = jnp.any((common > SHARED + 0.5) & (peer[:, None] != peer[None, :]))

    owner_of = wanted // own_blocks
    rank_of = jnp.sum(
        (owner_of[:, None] == owner_of[None, :]) & (jnp.arange(size)[None, :] < jnp.arange(size)[:, None]),
        axis=1,
    )
    lane = jnp.arange(CAP, dtype=jnp.int32)
    placed = (
        (owner_of[None, None, :] == peer[:, None, None]) & (rank_of[None, None, :] == lane[None, :, None])
    ).astype(f32)
    at_me = lists // own_blocks == me
    asked_at = before(at_me, 1)
    asked = (asked_at[:, None, :] == lane[None, :, None]) & at_me[:, None, :]
    local = jnp.arange(own_blocks, dtype=jnp.int32)
    here = (lists[:, :, None] - me * own_blocks) == local[None, None, :]
    back = jnp.einsum("irk,ikl->irl", asked.astype(f32), here.astype(f32))
    own_put = jnp.concatenate([jnp.zeros((owners, SHARED, own_blocks), f32), back], axis=1)
    own_put = own_put.reshape(owners * SLOTS, own_blocks)
    limit_pick = jnp.concatenate([jnp.zeros((owners, SHARED, size), f32), placed], axis=1)
    limit_pick = limit_pick.reshape(owners * SLOTS, size)
    placed = placed.reshape(owners * CAP, size)
    back = back.reshape(owners * CAP, own_blocks).T

    values = values_call(imp_vectors, mine, size)
    wide_pick = equal.astype(f32).reshape(owners * size, size)

    def wide(util):
        everyone = swap(jnp.broadcast_to(util[None], (owners, size, BLOCK)), "imp")
        return jnp.einsum("jk,jb->kb", wide_pick, everyone.reshape(owners * size, BLOCK), precision=HI)

    def combine_columns(ms):
        return swap(jnp.broadcast_to(ms[None], (columns,) + ms.shape), "ad")

    def exchange(send):
        return swap(send.reshape(owners, SLOTS, BLOCK), "imp").reshape(owners * SLOTS, BLOCK)

    flag = jnp.broadcast_to(crowded.astype(f32), (8, 128))
    ev, ms = score_call(first_score_kernel, values, [flag], 24, 0)
    every = combine_columns(ms)
    over = jnp.max(every[:, 16, 0]) > 0.5
    pick = jnp.where(over, 0.0, pick)
    util, send = utility_call(
        first_utility_kernel, ev, [ms, every, put, own_put, limits], (owners * SLOTS, BLOCK), False
    )
    recv = exchange(send)
    extra = lax.cond(over, wide, jnp.zeros_like, util)
    ev, ms, pace, wanted_limits = score_call(
        second_score_kernel, values, [util, recv, jnp.concatenate([pick, limit_pick], axis=1), extra], 16, 2
    )
    for step in range(2, ROUNDS):
        every = combine_columns(ms)
        util, send = utility_call(utility_kernel, ev, [ms, every, put], (owners * SLOTS, BLOCK), False)
        recv = exchange(send)
        extra = lax.cond(over, wide, jnp.zeros_like, util)
        ev, ms, pace = score_call(score_kernel, values, [util, recv, pick, extra, wanted_limits, pace], 16, 1)
    every = combine_columns(ms)
    util, send, prices = utility_call(
        last_utility_kernel, ev, [ms, every, placed, pace], (owners * CAP, 2 * BLOCK), True
    )
    recv = swap(send.reshape(owners, CAP, 2 * BLOCK), "imp").reshape(owners * CAP, 2 * BLOCK)
    final = pl.pallas_call(
        last_pace_kernel,
        out_shape=jax.ShapeDtypeStruct((own_blocks, BLOCK), f32),
        in_specs=[VMEM] * 3,
        out_specs=VMEM,
    )(recv, back, limits)
    return final.reshape(-1), prices.reshape(-1)


def solution(mesh):
    return jax.shard_map(
        per_device,
        mesh=mesh,
        in_specs=(P("imp", None), P(("imp", "ad"), None), P(("imp", "ad")), P("imp", "ad", None)),
        out_specs=(P(("imp", "ad")), P("imp")),
        check_vma=False,
    )
```

```python
import functools
import math

import jax
import jax.numpy as jnp
from jax import lax
from jax.experimental import pallas as pl
from jax.experimental.pallas import tpu as pltpu
from jax.sharding import PartitionSpec as P

BLOCK = 128
ROUNDS = 4
CAP = 2
SHARED = 6

softness_level = 0.5
util_floor = 0.01
pacing_cap = 3.0

LOG2E = math.log2(math.e)
LN2 = math.log(2.0)
SCALE = LOG2E / softness_level
HI = lax.Precision.HIGHEST
f32 = jnp.float32
bf16 = jnp.bfloat16
VMEM = pl.BlockSpec(memory_space=pltpu.VMEM)


def params(mib):
    return pltpu.CompilerParams(vmem_limit_bytes=mib * 2**20)


def pinned(x):
    return pltpu.with_memory_space_constraint(x, pltpu.VMEM)


def tn(a, b):
    return lax.dot_general(a, b, (((0,), (0,)), ((), ())), precision=HI, preferred_element_type=f32)


def nn(a, b):
    return lax.dot_general(a, b, (((1,), (0,)), ((), ())), precision=HI, preferred_element_type=f32)


def eye():
    return lax.broadcasted_iota(jnp.int32, (128, 128), 0) == lax.broadcasted_iota(
        jnp.int32, (128, 128), 1
    )


def spread_kernel(x_ref, out_ref, rows):
    half = out_ref.shape[0]
    own = out_ref.shape[1]
    rows[...] = x_ref[...].astype(f32)

    def one(p, _):
        for side in range(2):
            part = rows[pl.ds(p + side * half, own, stride=BLOCK), :]
            out_ref[p, :, side * 128 : (side + 1) * 128] = part.astype(bf16)
        return 0

    lax.fori_loop(0, half, one, 0)


def spread_call(ad_vectors):
    own = ad_vectors.shape[0] // BLOCK
    return pl.pallas_call(
        spread_kernel,
        out_shape=jax.ShapeDtypeStruct((BLOCK // 2, own, 256), bf16),
        in_specs=[VMEM],
        out_specs=VMEM,
        scratch_shapes=[pltpu.VMEM(ad_vectors.shape, f32)],
        compiler_params=params(24),
    )(ad_vectors)


def finish_score(v_ref, ev_ref, ms_ref, pace, sums, tops, highest):
    rows = v_ref.shape[0]
    chunks = rows // 128
    ms_ref[:, 0:chunks, :] = jnp.zeros((ms_ref.shape[0], chunks, 128), f32)

    @pl.when(jnp.logical_not(jnp.max(highest) < 2.0**90))
    def _():
        def body(step, _):
            at = pl.ds(pl.multiple_of(step * 8, 8), 8)
            v = v_ref[at, :]
            t = v * pace[...]
            m = jnp.max(t, axis=1, keepdims=True)
            e = jnp.exp2(t - m)
            ev_ref[at, :] = e * v
            tops[at, :] = jnp.broadcast_to(m, (8, 128))
            lane = lax.broadcasted_iota(jnp.int32, (8, 128), 1)
            sums[at, :] = jnp.where(lane == 0, jnp.sum(e, axis=1, keepdims=True), 0.0)
            return 0

        lax.fori_loop(0, rows // 8, body, 0)
        for c in range(chunks):
            row = jnp.sum(jnp.where(eye(), tops[c * 128 : (c + 1) * 128, :], 0.0), axis=0, keepdims=True)
            for a in range(ms_ref.shape[0]):
                ms_ref[a, c : c + 1, :] = row

    total = lax.dot_general(
        jnp.ones((8, 128), f32), sums[...], (((1,), (1,)), ((), ())), precision=HI, preferred_element_type=f32
    )
    for c in range(chunks):
        for a in range(ms_ref.shape[0]):
            ms_ref[a, chunks + c : chunks + c + 1, :] = total[0:1, c * 128 : (c + 1) * 128]


def values_kernel(blocks, x_ref, y_ref, v_ref, ev_ref, ms_ref, ya, yb, yt, pace, sums, tops):
    parts = y_ref.shape[0] // blocks
    ya[...] = y_ref[:, :128].astype(f32)
    yb[...] = y_ref[:, 128:].astype(f32)

    def unpack(k, _):
        at = pl.multiple_of(k * BLOCK, BLOCK)
        yt[pl.ds(at, parts), :] = ya[pl.ds(k, parts, stride=blocks), :].astype(bf16)
        yt[pl.ds(at + parts, parts), :] = yb[pl.ds(k, parts, stride=blocks), :].astype(bf16)
        return 0

    lax.fori_loop(0, blocks, unpack, 0)
    rows = x_ref.shape[0]
    tile_c = 1024
    sums[...] = jnp.zeros(sums.shape, f32)

    def tile(step, _):
        cols = pl.ds(pl.multiple_of(step * tile_c, tile_c), tile_c)
        s = lax.dot_general(
            x_ref[...], yt[cols, :], (((1,), (1,)), ((), ())), preferred_element_type=f32
        )
        v = jnp.maximum(s, 0.0) + jnp.log(1.0 + jnp.exp2(jnp.abs(s) * -LOG2E))
        e = jnp.exp2(v * SCALE)
        v_ref[:, cols] = v
        ev_ref[:, cols] = e * v
        part = e[:, 0:128]
        for k in range(1, tile_c // 128):
            part = part + e[:, k * 128 : (k + 1) * 128]
        sums[...] += part
        return 0

    lax.fori_loop(0, v_ref.shape[1] // tile_c, tile, 0)
    pace[...] = jnp.full(pace.shape, SCALE, f32)
    highest = jnp.max(sums[...].reshape(rows // 8, 8, 128), axis=0)
    finish_score(v_ref, ev_ref, ms_ref, pace, sums, tops, highest)


def score_scratch(rows, width):
    return [pltpu.VMEM((8, width), f32), pltpu.VMEM((rows, 128), f32), pltpu.VMEM((rows, 128), f32)]


def values_call(x, y, blocks, columns):
    rows, width = x.shape[0], blocks * BLOCK
    return pl.pallas_call(
        functools.partial(values_kernel, blocks),
        out_shape=[
            pltpu.VMEM((rows, width), f32),
            pltpu.VMEM((rows, width), f32),
            jax.ShapeDtypeStruct((columns, rows // 64, 128), f32),
        ],
        in_specs=[VMEM, VMEM],
        out_specs=[VMEM] * 3,
        scratch_shapes=[
            pltpu.VMEM((y.shape[0], 128), f32),
            pltpu.VMEM((y.shape[0], 128), f32),
            pltpu.VMEM((width, 128), bf16),
        ]
        + score_scratch(rows, width),
        compiler_params=params(24),
    )(x, y)


def score(v_ref, ev_ref, ms_ref, pace, sums, tops):
    rows, width = v_ref.shape
    step_rows = 128

    def body(step, highest):
        base = pl.multiple_of(step * step_rows, step_rows)
        total = [None] * (step_rows // 8)
        for k in range(width // 128):
            cols = slice(k * 128, (k + 1) * 128)
            scale = pace[:, cols]
            for part in range(step_rows // 8):
                v = v_ref[pl.ds(base + part * 8, 8), cols]
                e = jnp.exp2(v * scale)
                ev_ref[pl.ds(base + part * 8, 8), cols] = e * v
                total[part] = e if k == 0 else total[part] + e
        for part in range(step_rows // 8):
            sums[pl.ds(base + part * 8, 8), :] = total[part]
            highest = jnp.maximum(highest, total[part])
        return highest

    highest = lax.fori_loop(0, rows // step_rows, body, jnp.zeros((8, 128), f32))
    finish_score(v_ref, ev_ref, ms_ref, pace, sums, tops, highest)


def pace_step(pace, util, limit):
    return jnp.sqrt(pace * jnp.minimum(limit / jnp.maximum(util, util_floor), pacing_cap))


def spread_pace(p, pace):
    for k in range(p.shape[0]):
        pace[:, k * BLOCK : (k + 1) * BLOCK] = jnp.broadcast_to(p[k : k + 1, :] * SCALE, (8, BLOCK))


def second_score_kernel(
    util_ref, recv_ref, pick_ref, v_in, ev_in, v_ref, ev_ref, ms_ref, p_ref, limit_ref, pace, sums, tops
):
    blocks = util_ref.shape[0]
    got = tn(pick_ref[...], recv_ref[...].reshape(-1, BLOCK))
    limit = got[blocks:, :]
    p = pace_step(jnp.ones(limit.shape, f32), util_ref[...] + got[:blocks, :], limit)
    p_ref[...] = p
    limit_ref[...] = limit
    spread_pace(p, pace)
    score(v_in, ev_ref, ms_ref, pace, sums, tops)


def score_kernel(
    util_ref, recv_ref, pick_ref, limit_ref, old_ref, v_in, ev_in, v_ref, ev_ref, ms_ref, p_ref, pace, sums, tops
):
    util = util_ref[...] + tn(pick_ref[...], recv_ref[...].reshape(-1, BLOCK))
    p = pace_step(old_ref[...], util, limit_ref[...])
    p_ref[...] = p
    spread_pace(p, pace)
    score(v_in, ev_ref, ms_ref, pace, sums, tops)


def score_call(kernel, v, ev, args, columns, outs):
    rows, width = v.shape
    small = jax.ShapeDtypeStruct((width // BLOCK, BLOCK), f32)
    return pl.pallas_call(
        kernel,
        out_shape=[
            pltpu.VMEM((rows, width), f32),
            pltpu.VMEM((rows, width), f32),
            jax.ShapeDtypeStruct((columns, rows // 64, 128), f32),
        ]
        + [small] * outs,
        in_specs=[VMEM] * (len(args) + 2),
        out_specs=[VMEM] * (3 + outs),
        scratch_shapes=score_scratch(rows, width),
        input_output_aliases={len(args): 0, len(args) + 1: 1},
        compiler_params=params(24),
    )(*args, pinned(v), pinned(ev))


def combine(ms_ref, all_ref):
    chunks = ms_ref.shape[1] // 2
    tops = all_ref[:, 0:chunks, :]
    sums = all_ref[:, chunks : 2 * chunks, :]
    top = jnp.max(tops, axis=0)
    total = jnp.sum(sums * jnp.exp2(tops - top[None]), axis=0)
    lse = top + LOG2E * jnp.log(total)
    return lse, jnp.exp2(ms_ref[0, 0:chunks, :] - lse)


def utility(weight, ev_ref, util_ref, wcol):
    rows, width = ev_ref.shape
    for c in range(rows // 128):
        spread = jnp.where(eye(), jnp.broadcast_to(weight[c : c + 1, :], (128, 128)), 0.0)
        wcol[c * 128 : (c + 1) * 128, :] = jnp.broadcast_to(
            jnp.sum(spread, axis=1, keepdims=True), (128, 128)
        )
    blocks = width // BLOCK
    step_rows = 128

    def body(step, acc):
        out = list(acc)
        base = pl.multiple_of(step * step_rows, step_rows)
        for part in range(step_rows // 8):
            at = pl.ds(base + part * 8, 8)
            w = wcol[at, :]
            for k in range(blocks):
                out[k] = out[k] + ev_ref[at, k * BLOCK : (k + 1) * BLOCK] * w
        return tuple(out)

    acc = lax.fori_loop(
        0, rows // step_rows, body, tuple(jnp.zeros((8, BLOCK), f32) for _ in range(blocks))
    )
    for k in range(blocks):
        util_ref[k : k + 1, :] = jnp.sum(acc[k], axis=0, keepdims=True)


def utility_kernel(first, ms_ref, all_ref, put_ref, *refs):
    refs = list(refs)
    if first:
        own_put_ref, limit_ref = refs[:2]
        refs = refs[2:]
    v_in, ev_in, v_ref, ev_ref, util_ref, send_ref, wcol = refs
    _, weight = combine(ms_ref, all_ref)
    utility(weight, ev_in, util_ref, wcol)
    send = nn(put_ref[...], util_ref[...])
    if first:
        send = send + nn(own_put_ref[...], limit_ref[...])
    send_ref[...] = send.reshape(send_ref.shape)


def last_utility_kernel(ms_ref, all_ref, put_ref, p_ref, v_in, ev_in, v_ref, ev_ref, both_ref, send_ref, price_ref, wcol):
    lse, weight = combine(ms_ref, all_ref)
    price_ref[...] = lse * (softness_level * LN2)
    blocks = p_ref.shape[0]
    utility(weight, ev_in, both_ref, wcol)
    both_ref[blocks:, :] = p_ref[...]
    send_ref[...] = nn(put_ref[...], both_ref[...]).reshape(send_ref.shape)


def utility_call(kernel, v, ev, args, util_rows, send_shape, price):
    rows, width = ev.shape
    outs = [
        pltpu.VMEM((rows, width), f32),
        pltpu.VMEM((rows, width), f32),
        jax.ShapeDtypeStruct((util_rows, BLOCK), f32),
        jax.ShapeDtypeStruct(send_shape, f32),
    ]
    if price:
        outs.append(jax.ShapeDtypeStruct((rows // 128, 128), f32))
    return pl.pallas_call(
        kernel,
        out_shape=outs,
        in_specs=[VMEM] * (len(args) + 2),
        out_specs=[VMEM] * len(outs),
        scratch_shapes=[pltpu.VMEM((rows, 128), f32)],
        input_output_aliases={len(args): 0, len(args) + 1: 1},
        compiler_params=params(24),
    )(*args, pinned(v), pinned(ev))


def last_pace_kernel(recv_ref, back_ref, limit_ref, out_ref):
    limit = limit_ref[...]
    own = limit.shape[0]
    back = back_ref[...]
    got = nn(back, recv_ref[...].reshape(-1, BLOCK))
    count = jnp.sum(back[own:, :], axis=1, keepdims=True)
    lone = jnp.ones(limit.shape, f32)
    for _ in range(ROUNDS - 1):
        lone = pace_step(lone, jnp.zeros(limit.shape, f32), limit)
    pace = jnp.where(count > 0.0, got[own:, :] / jnp.maximum(count, 1.0), lone)
    out_ref[...] = pace_step(pace, got[:own, :], limit)


def before(flags, axis):
    size = flags.shape[axis]
    order = jnp.arange(size)
    less = (order[:, None] < order[None, :]).astype(f32)
    moved = jnp.moveaxis(flags, axis, -1).astype(f32)
    return jnp.moveaxis(jnp.dot(moved, less), -1, axis).astype(jnp.int32)


def swap(x, axis):
    return lax.all_to_all(x, axis, split_axis=0, concat_axis=0, tiled=True)


def share_plan(lists, wanted, equal, placed, back, shared):
    owners, size = lists.shape
    own_blocks = back.shape[2]
    gives = jnp.any(equal, axis=1)
    takes = jnp.any(equal, axis=2)
    slot = jnp.arange(shared, dtype=jnp.int32)[None, :, None]
    put = ((before(gives, 1)[:, None, :] == slot) & gives[:, None, :]).astype(f32)
    take_slot = ((before(takes, 1)[:, None, :] == slot) & takes[:, None, :]).astype(f32)
    pick = jnp.einsum("isk,ikw->isw", take_slot, equal.astype(f32))
    slots = shared + CAP

    def pad(x, low, high):
        return jnp.pad(x, ((0, 0), (low, high), (0, 0))).reshape(owners * slots, x.shape[2])

    put, pick = pad(put, 0, CAP), pad(pick, 0, CAP)
    own_put, limit_pick = pad(back, shared, 0), pad(placed, shared, 0)
    return put, pick, own_put, jnp.concatenate([pick, limit_pick], axis=1)


def rounds(columns, shared, imp_vectors, mine, limits, plan, last_put, last_back):
    put, pick, own_put, first_pick = plan
    size = put.shape[1]
    owners = put.shape[0] // (shared + CAP)
    shape = (owners, shared + CAP, BLOCK)
    v, ev, ms = values_call(imp_vectors, mine, size, columns)
    every = swap(ms, "ad")
    v, ev, util, send = utility_call(
        functools.partial(utility_kernel, True), v, ev, [ms, every, put, own_put, limits], size, shape, False
    )
    recv = swap(send, "imp")
    v, ev, ms, pace, wanted_limits = score_call(
        second_score_kernel, v, ev, [util, recv, first_pick], columns, 2
    )
    for step in range(2, ROUNDS):
        every = swap(ms, "ad")
        v, ev, util, send = utility_call(
            functools.partial(utility_kernel, False), v, ev, [ms, every, put], size, shape, False
        )
        recv = swap(send, "imp")
        v, ev, ms, pace = score_call(
            score_kernel, v, ev, [util, recv, pick, wanted_limits, pace], columns, 1
        )
    every = swap(ms, "ad")
    _, _, _, send, prices = utility_call(
        last_utility_kernel, v, ev, [ms, every, last_put, pace], 2 * size, (owners, 2 * CAP, BLOCK), True
    )
    recv = swap(send, "imp")
    final = pl.pallas_call(
        last_pace_kernel,
        out_shape=jax.ShapeDtypeStruct(limits.shape, f32),
        in_specs=[VMEM] * 3,
        out_specs=VMEM,
    )(recv, last_back, limits)
    return final, prices


def per_device(imp_vectors, ad_vectors, spend_limits, targets):
    owners = lax.axis_size("imp")
    columns = lax.axis_size("ad")
    me = lax.axis_index("imp")
    emb = imp_vectors.shape[1]
    own_blocks = ad_vectors.shape[0] // BLOCK
    wanted = targets.reshape(-1)
    size = wanted.shape[0]
    limits = spend_limits.reshape(own_blocks, BLOCK)

    lists = swap(jnp.broadcast_to(wanted[None, :], (owners, size)), "imp")
    table = swap(spread_call(ad_vectors), "imp").reshape(owners * own_blocks, 2 * emb)
    chosen = table[lists.reshape(-1)].reshape(owners, size, 2 * emb)
    mine = swap(chosen, "imp").reshape(owners * size, 2 * emb)

    peer = jnp.arange(owners, dtype=jnp.int32)
    equal = (lists[:, :, None] == wanted[None, None, :]) & (peer != me)[:, None, None]
    owner_of = wanted // own_blocks
    rank_of = jnp.sum(
        (owner_of[:, None] == owner_of[None, :]) & (jnp.arange(size)[None, :] < jnp.arange(size)[:, None]),
        axis=1,
    )
    lane = jnp.arange(CAP, dtype=jnp.int32)
    placed = (
        (owner_of[None, None, :] == peer[:, None, None]) & (rank_of[None, None, :] == lane[None, :, None])
    ).astype(f32)
    at_me = lists // own_blocks == me
    asked = (before(at_me, 1)[:, None, :] == lane[None, :, None]) & at_me[:, None, :]
    local = jnp.arange(own_blocks, dtype=jnp.int32)
    here = (lists[:, :, None] - me * own_blocks) == local[None, None, :]
    back = jnp.einsum("irk,ikl->irl", asked.astype(f32), here.astype(f32))

    def doubled(x):
        none = jnp.zeros_like(x)
        both = jnp.concatenate(
            [jnp.concatenate([x, none], axis=2), jnp.concatenate([none, x], axis=2)], axis=1
        )
        return both.reshape(owners * 2 * CAP, 2 * x.shape[2])

    last_put, last_back = doubled(placed), doubled(back).T
    narrow = share_plan(lists, wanted, equal, placed, back, SHARED)

    holds = jnp.any(
        lists[:, :, None] == jnp.arange(owners * own_blocks, dtype=jnp.int32)[None, None, :], axis=1
    ).astype(bf16)
    common = lax.dot_general(holds, holds, (((1,), (1,)), ((), ())), preferred_element_type=f32)
    crowded = jnp.any((common > SHARED + 0.5) & (peer[:, None] != peer[None, :]))
    over = lax.pmax(crowded.astype(f32), "ad") > 0.5
    mine, narrow, last_put, last_back = lax.optimization_barrier((mine, narrow, last_put, last_back))

    def take_narrow():
        return rounds(columns, SHARED, imp_vectors, mine, limits, narrow, last_put, last_back)

    def take_wide():
        plan = share_plan(lists, wanted, equal, placed, back, size)
        return rounds(columns, size, imp_vectors, mine, limits, plan, last_put, last_back)

    final, prices = lax.cond(over, take_wide, take_narrow)
    return final.reshape(-1), prices.reshape(-1)


def solution(mesh):
    return jax.shard_map(
        per_device,
        mesh=mesh,
        in_specs=(P("imp", None), P(("imp", "ad"), None), P(("imp", "ad")), P("imp", "ad", None)),
        out_specs=(P(("imp", "ad")), P("imp")),
        check_vma=False,
    )
```

```python
import functools
import math

import jax
import jax.numpy as jnp
from jax import lax
from jax.experimental import pallas as pl
from jax.experimental.pallas import tpu as pltpu
from jax.sharding import PartitionSpec as P

BLOCK = 128
ROUNDS = 4
CAP = 2
SHARED = 6

softness_level = 0.5
util_floor = 0.01
pacing_cap = 3.0

LOG2E = math.log2(math.e)
LN2 = math.log(2.0)
SCALE = LOG2E / softness_level
SAFE = 2.0**90
HI = lax.Precision.HIGHEST
f32 = jnp.float32
bf16 = jnp.bfloat16
VMEM = pl.BlockSpec(memory_space=pltpu.VMEM)
SMEM = pl.BlockSpec(memory_space=pltpu.SMEM)


def params():
    return pltpu.CompilerParams(vmem_limit_bytes=24 * 2**20)


def pinned(x):
    return pltpu.with_memory_space_constraint(x, pltpu.VMEM)


def select(chooser, x):
    high = x.astype(bf16)
    rest = x - high.astype(f32)
    mid = rest.astype(bf16)
    low = (rest - mid.astype(f32)).astype(bf16)
    terms = jnp.concatenate([high, mid, low], axis=1)
    out = lax.dot_general(chooser, terms, (((1,), (0,)), ((), ())), preferred_element_type=f32)
    n = x.shape[1]
    return out[:, :n] + out[:, n : 2 * n] + out[:, 2 * n :]


def eye():
    return lax.broadcasted_iota(jnp.int32, (128, 128), 0) == lax.broadcasted_iota(
        jnp.int32, (128, 128), 1
    )


def gather_kernel(index_ref, table_ref, out_ref):
    group = 32

    def some(step, _):
        for j in range(group):
            at = step * group + j
            out_ref[at] = table_ref[index_ref[at]]
        return 0

    lax.fori_loop(0, out_ref.shape[0] // group, some, 0)


def gather_call(index, table):
    return pl.pallas_call(
        gather_kernel,
        out_shape=jax.ShapeDtypeStruct(index.shape + table.shape[1:], table.dtype),
        in_specs=[SMEM, VMEM],
        out_specs=VMEM,
        compiler_params=params(),
    )(index, table)


def finish_score(v_ref, ms_ref, pace, sums, tops, highest):
    rows = v_ref.shape[0]
    chunks = rows // 128
    ms_ref[0:chunks, :] = jnp.zeros((chunks, 128), f32)

    @pl.when(jnp.logical_not(highest < SAFE))
    def _():
        lane = lax.broadcasted_iota(jnp.int32, (8, 128), 1)

        def body(step, _):
            at = pl.ds(pl.multiple_of(step * 8, 8), 8)
            t = v_ref[at, :] * pace[...]
            m = jnp.max(t, axis=1, keepdims=True)
            total = jnp.sum(jnp.exp2(t - m), axis=1, keepdims=True)
            tops[at, :] = jnp.broadcast_to(m, (8, 128))
            sums[at, :] = jnp.where(lane == 0, total, 0.0)
            return 0

        lax.fori_loop(0, rows // 8, body, 0)
        for c in range(chunks):
            ms_ref[c : c + 1, :] = jnp.sum(
                jnp.where(eye(), tops[c * 128 : (c + 1) * 128, :], 0.0), axis=0, keepdims=True
            )

    total = lax.dot_general(
        jnp.ones((8, 128), f32), sums[...], (((1,), (1,)), ((), ())), precision=HI, preferred_element_type=f32
    )
    for c in range(chunks):
        ms_ref[chunks + c : chunks + c + 1, :] = total[0:1, c * 128 : (c + 1) * 128]


def values_kernel(blocks, x_ref, y_ref, v_ref, ms_ref, wide, yt, pace, sums, tops):
    half = BLOCK // 2
    wide[...] = y_ref[...].astype(f32)
    for k in range(blocks):
        for side in range(2):
            at = k * BLOCK + side * half
            yt[at : at + half, :] = wide[pl.ds(2 * k + side, half, stride=2 * blocks), :].astype(bf16)
    tile_c = 1024
    tiles = v_ref.shape[1] // tile_c
    sums[...] = jnp.zeros(sums.shape, f32)

    def product(step):
        cols = pl.ds(pl.multiple_of(step * tile_c, tile_c), tile_c)
        return cols, lax.dot_general(
            x_ref[...], yt[cols, :], (((1,), (1,)), ((), ())), preferred_element_type=f32
        )

    def tile(step, _):
        cols, s = product(step)
        grown = 1.0 + jnp.exp2(s * LOG2E)
        v_ref[:, cols] = jnp.log(grown)
        e = grown * grown
        part = e[:, 0:128]
        for k in range(1, tile_c // 128):
            part = part + e[:, k * 128 : (k + 1) * 128]
        sums[...] += part
        return 0

    lax.fori_loop(0, tiles, tile, 0)
    highest = jnp.max(sums[...])

    @pl.when(jnp.logical_not(highest < SAFE))
    def _():
        def again(step, _):
            cols, s = product(step)
            v_ref[:, cols] = jnp.maximum(s, 0.0) + jnp.log(1.0 + jnp.exp2(jnp.abs(s) * -LOG2E))
            return 0

        lax.fori_loop(0, tiles, again, 0)
        pace[...] = jnp.full(pace.shape, SCALE, f32)

    finish_score(v_ref, ms_ref, pace, sums, tops, highest)


def score_scratch(rows, width):
    return [pltpu.VMEM((8, width), f32), pltpu.VMEM((rows, 128), f32), pltpu.VMEM((rows, 128), f32)]


def values_call(x, y, blocks):
    rows, width = x.shape[0], blocks * BLOCK
    return pl.pallas_call(
        functools.partial(values_kernel, blocks),
        out_shape=[
            pltpu.VMEM((rows, width), f32),
            jax.ShapeDtypeStruct((rows // 64, 128), f32),
        ],
        in_specs=[VMEM, VMEM],
        out_specs=[VMEM] * 2,
        scratch_shapes=[pltpu.VMEM(y.shape, f32), pltpu.VMEM(y.shape, bf16)] + score_scratch(rows, width),
        compiler_params=params(),
    )(x, y)


def score(v_ref, ms_ref, pace, sums, tops):
    rows, width = v_ref.shape
    step_rows = 128

    def body(step, highest):
        base = pl.multiple_of(step * step_rows, step_rows)
        total = [None] * (step_rows // 8)
        for k in range(width // 128):
            cols = slice(k * 128, (k + 1) * 128)
            scale = pace[:, cols]
            for part in range(step_rows // 8):
                e = jnp.exp2(v_ref[pl.ds(base + part * 8, 8), cols] * scale)
                total[part] = e if k == 0 else total[part] + e
        for part in range(step_rows // 8):
            sums[pl.ds(base + part * 8, 8), :] = total[part]
            highest = jnp.maximum(highest, total[part])
        return highest

    highest = lax.fori_loop(0, rows // step_rows, body, jnp.zeros((8, 128), f32))
    finish_score(v_ref, ms_ref, pace, sums, tops, jnp.max(highest))


def pace_step(pace, util, limit):
    return jnp.sqrt(pace * jnp.minimum(limit / jnp.maximum(util, util_floor), pacing_cap))


def spread_pace(p, pace):
    for k in range(p.shape[0]):
        pace[:, k * BLOCK : (k + 1) * BLOCK] = jnp.broadcast_to(p[k : k + 1, :] * SCALE, (8, BLOCK))


def second_score_kernel(util_ref, recv_ref, pick_ref, v_in, v_ref, ms_ref, p_ref, limit_ref, pace, sums, tops):
    blocks = util_ref.shape[0]
    got = select(pick_ref[...], recv_ref[...].reshape(-1, BLOCK))
    limit = got[blocks:, :]
    p = pace_step(jnp.ones(limit.shape, f32), util_ref[...] + got[:blocks, :], limit)
    p_ref[...] = p
    limit_ref[...] = limit
    spread_pace(p, pace)
    score(v_in, ms_ref, pace, sums, tops)


def score_kernel(util_ref, recv_ref, pick_ref, limit_ref, old_ref, v_in, v_ref, ms_ref, p_ref, pace, sums, tops):
    util = util_ref[...] + select(pick_ref[...], recv_ref[...].reshape(-1, BLOCK))
    p = pace_step(old_ref[...], util, limit_ref[...])
    p_ref[...] = p
    spread_pace(p, pace)
    score(v_in, ms_ref, pace, sums, tops)


def score_call(kernel, v, args, outs):
    rows, width = v.shape
    small = jax.ShapeDtypeStruct((width // BLOCK, BLOCK), f32)
    return pl.pallas_call(
        kernel,
        out_shape=[pltpu.VMEM((rows, width), f32), jax.ShapeDtypeStruct((rows // 64, 128), f32)]
        + [small] * outs,
        in_specs=[VMEM] * (len(args) + 1),
        out_specs=[VMEM] * (2 + outs),
        scratch_shapes=score_scratch(rows, width),
        input_output_aliases={len(args): 0},
        compiler_params=params(),
    )(*args, pinned(v))


def combine(ms_refs):
    chunks = ms_refs[0].shape[0] // 2
    top = functools.reduce(jnp.maximum, [ref[0:chunks, :] for ref in ms_refs])
    total = sum(ref[chunks:, :] * jnp.exp2(ref[0:chunks, :] - top) for ref in ms_refs)
    return top + LOG2E * jnp.log(total)


def utility(lse, v_ref, util_ref, pace, column):
    rows, width = v_ref.shape
    for c in range(rows // 128):
        column[c * 128 : (c + 1) * 128, :] = jnp.transpose(jnp.broadcast_to(lse[c : c + 1, :], (128, 128)))
    blocks = width // BLOCK
    step_rows = 128

    def body(step, _):
        base = pl.multiple_of(step * step_rows, step_rows)
        for k in range(blocks):
            cols = slice(k * BLOCK, (k + 1) * BLOCK)
            scale = pace[:, cols]
            acc = None
            for part in range(step_rows // 8):
                at = pl.ds(base + part * 8, 8)
                v = v_ref[at, cols]
                term = jnp.exp2(v * scale - column[at, :]) * v
                acc = term if acc is None else acc + term
            util_ref[k : k + 1, :] += jnp.sum(acc, axis=0, keepdims=True)
        return 0

    util_ref[0:blocks, :] = jnp.zeros((blocks, BLOCK), f32)
    lax.fori_loop(0, rows // step_rows, body, 0)


def utility_kernel(columns, first, *refs):
    ms_refs, refs = refs[:columns], refs[columns:]
    if first:
        put_ref, own_put_ref, limit_ref, v_in, v_ref, util_ref, send_ref, pace, column = refs
        pace[...] = jnp.full(pace.shape, SCALE, f32)
    else:
        put_ref, p_ref, v_in, v_ref, util_ref, send_ref, pace, column = refs
        spread_pace(p_ref[...], pace)
    utility(combine(ms_refs), v_in, util_ref, pace, column)
    send = select(put_ref[...], util_ref[...])
    if first:
        send = send + select(own_put_ref[...], limit_ref[...])
    send_ref[...] = send.reshape(send_ref.shape)


def last_utility_kernel(columns, *refs):
    ms_refs, refs = refs[:columns], refs[columns:]
    put_ref, p_ref, v_in, v_ref, both_ref, send_ref, price_ref, pace, column = refs
    lse = combine(ms_refs)
    price_ref[...] = lse * (softness_level * LN2)
    blocks = p_ref.shape[0]
    spread_pace(p_ref[...], pace)
    utility(lse, v_in, both_ref, pace, column)
    both_ref[blocks:, :] = p_ref[...]
    send_ref[...] = select(put_ref[...], both_ref[...]).reshape(send_ref.shape)


def utility_call(kernel, v, args, util_rows, send_shape, price):
    rows, width = v.shape
    outs = [
        pltpu.VMEM((rows, width), f32),
        jax.ShapeDtypeStruct((util_rows, BLOCK), f32),
        jax.ShapeDtypeStruct(send_shape, f32),
    ]
    if price:
        outs.append(jax.ShapeDtypeStruct((rows // 128, 128), f32))
    return pl.pallas_call(
        kernel,
        out_shape=outs,
        in_specs=[VMEM] * (len(args) + 1),
        out_specs=[VMEM] * len(outs),
        scratch_shapes=[pltpu.VMEM((8, width), f32), pltpu.VMEM((rows, 128), f32)],
        input_output_aliases={len(args): 0},
        compiler_params=params(),
    )(*args, pinned(v))


def last_pace_kernel(recv_ref, back_ref, limit_ref, out_ref):
    limit = limit_ref[...]
    own = limit.shape[0]
    back = back_ref[...]
    got = select(back, recv_ref[...].reshape(-1, BLOCK))
    count = jnp.sum(back[own:, :].astype(f32), axis=1, keepdims=True)
    lone = jnp.ones(limit.shape, f32)
    for _ in range(ROUNDS - 1):
        lone = pace_step(lone, jnp.zeros(limit.shape, f32), limit)
    pace = jnp.where(count > 0.0, got[own:, :] / jnp.maximum(count, 1.0), lone)
    out_ref[...] = pace_step(pace, got[:own, :], limit)


def before(flags, axis):
    size = flags.shape[axis]
    order = jnp.arange(size)
    less = (order[:, None] < order[None, :]).astype(f32)
    moved = jnp.moveaxis(flags, axis, -1).astype(f32)
    return jnp.moveaxis(jnp.dot(moved, less), -1, axis).astype(jnp.int32)


def swap(x, axis):
    return lax.all_to_all(x, axis, split_axis=0, concat_axis=0, tiled=True)


def share_plan(equal, placed, back, shared):
    owners = equal.shape[0]
    gives = jnp.any(equal, axis=1)
    takes = jnp.any(equal, axis=2)
    slot = jnp.arange(shared, dtype=jnp.int32)[None, :, None]
    put = ((before(gives, 1)[:, None, :] == slot) & gives[:, None, :]).astype(f32)
    take_slot = ((before(takes, 1)[:, None, :] == slot) & takes[:, None, :]).astype(f32)
    pick = jnp.einsum("isk,ikw->isw", take_slot, equal.astype(f32))
    slots = shared + CAP

    def pad(x, low, high):
        return jnp.pad(x.astype(bf16), ((0, 0), (low, high), (0, 0))).reshape(owners * slots, x.shape[2])

    put, pick = pad(put, 0, CAP), pad(pick, 0, CAP).T
    own_put, limit_pick = pad(back, shared, 0), pad(placed, shared, 0).T
    return put, pick, own_put, jnp.concatenate([pick, limit_pick], axis=0)


def rounds(columns, shared, imp_vectors, mine, limits, plan, last_put, last_back):
    put, pick, own_put, first_pick = plan
    size = put.shape[1]
    owners = put.shape[0] // (shared + CAP)
    shape = (owners, shared + CAP, BLOCK)

    def everywhere(ms):
        shifts = sorted(range(1, columns), key=lambda d: -min(d, columns - d))
        return [ms] + [
            lax.ppermute(ms, "ad", [(i, (i + d) % columns) for i in range(columns)]) for d in shifts
        ]

    v, ms = values_call(imp_vectors, mine, size)
    v, util, send = utility_call(
        functools.partial(utility_kernel, columns, True),
        v, everywhere(ms) + [put, own_put, limits], size, shape, False,
    )
    recv = swap(send, "imp")
    v, ms, pace, wanted_limits = score_call(second_score_kernel, v, [util, recv, first_pick], 2)
    for step in range(2, ROUNDS):
        v, util, send = utility_call(
            functools.partial(utility_kernel, columns, False), v, everywhere(ms) + [put, pace], size, shape, False
        )
        recv = swap(send, "imp")
        v, ms, pace = score_call(score_kernel, v, [util, recv, pick, wanted_limits, pace], 1)
    _, _, send, prices = utility_call(
        functools.partial(last_utility_kernel, columns),
        v, everywhere(ms) + [last_put, pace], 2 * size, (owners, 2 * CAP, BLOCK), True,
    )
    recv = swap(send, "imp")
    final = pl.pallas_call(
        last_pace_kernel,
        out_shape=jax.ShapeDtypeStruct(limits.shape, f32),
        in_specs=[VMEM] * 3,
        out_specs=VMEM,
        compiler_params=params(),
    )(recv, last_back, limits)
    return final, prices


def per_device(imp_vectors, ad_vectors, spend_limits, targets):
    owners = lax.axis_size("imp")
    columns = lax.axis_size("ad")
    me = lax.axis_index("imp")
    emb = imp_vectors.shape[1]
    own_blocks = ad_vectors.shape[0] // BLOCK
    wanted = targets.reshape(-1)
    size = wanted.shape[0]
    limits = spend_limits.reshape(own_blocks, BLOCK)
    half = BLOCK // 2

    lists = swap(jnp.broadcast_to(wanted[None, :], (owners, size)), "imp")
    pieces = ad_vectors.reshape(own_blocks, 2, half, emb).transpose(2, 0, 1, 3)
    table = swap(pieces, "imp").reshape(owners * own_blocks, 2, emb)
    chosen = gather_call(lists.reshape(-1), table).reshape(owners, size, 2, emb)
    mine = swap(chosen, "imp").reshape(owners * size * 2, emb)

    peer = jnp.arange(owners, dtype=jnp.int32)
    equal = (lists[:, :, None] == wanted[None, None, :]) & (peer != me)[:, None, None]
    owner_of = wanted // own_blocks
    rank_of = jnp.sum(
        (owner_of[:, None] == owner_of[None, :]) & (jnp.arange(size)[None, :] < jnp.arange(size)[:, None]),
        axis=1,
    )
    lane = jnp.arange(CAP, dtype=jnp.int32)
    placed = (
        (owner_of[None, None, :] == peer[:, None, None]) & (rank_of[None, None, :] == lane[None, :, None])
    ).astype(f32)
    at_me = lists // own_blocks == me
    asked = (before(at_me, 1)[:, None, :] == lane[None, :, None]) & at_me[:, None, :]
    local = jnp.arange(own_blocks, dtype=jnp.int32)
    here = (lists[:, :, None] - me * own_blocks) == local[None, None, :]
    back = jnp.einsum("irk,ikl->irl", asked.astype(f32), here.astype(f32))

    def doubled(x):
        none = jnp.zeros_like(x)
        both = jnp.concatenate(
            [jnp.concatenate([x, none], axis=2), jnp.concatenate([none, x], axis=2)], axis=1
        )
        return both.reshape(owners * 2 * CAP, 2 * x.shape[2]).astype(bf16)

    last_put, last_back = doubled(placed), doubled(back).T
    narrow = share_plan(equal, placed, back, SHARED)

    holds = jnp.any(
        lists[:, :, None] == jnp.arange(owners * own_blocks, dtype=jnp.int32)[None, None, :], axis=1
    ).astype(bf16)
    common = lax.dot_general(holds, holds, (((1,), (1,)), ((), ())), preferred_element_type=f32)
    crowded = jnp.any((common > SHARED + 0.5) & (peer[:, None] != peer[None, :]))
    over = lax.pmax(crowded.astype(f32), "ad")
    mine, narrow, last_put, last_back, over = lax.optimization_barrier(
        (mine, narrow, last_put, last_back, over)
    )

    final, prices = rounds(columns, SHARED, imp_vectors, mine, limits, narrow, last_put, last_back)

    def take_wide():
        plan = share_plan(equal, placed, back, size)
        return rounds(columns, size, imp_vectors, mine, limits, plan, last_put, last_back)

    final, prices = lax.cond(over > 0.5, take_wide, lambda: (final, prices))
    return final.reshape(-1), prices.reshape(-1)


def solution(mesh):
    return jax.shard_map(
        per_device,
        mesh=mesh,
        in_specs=(P("imp", None), P(("imp", "ad"), None), P(("imp", "ad")), P("imp", "ad", None)),
        out_specs=(P(("imp", "ad")), P("imp")),
        check_vma=False,
    )
```

```python
import functools
import math

import jax
import jax.numpy as jnp
from jax import lax
from jax.experimental import pallas as pl
from jax.experimental.layout import Layout, with_layout_constraint
from jax.experimental.pallas import tpu as pltpu
from jax.sharding import PartitionSpec as P

BLOCK = 128
ROUNDS = 4
CAP = 2
SHARED = 8

softness_level = 0.5
util_floor = 0.01
pacing_cap = 3.0

LOG2E = math.log2(math.e)
LN2 = math.log(2.0)
SCALE = LOG2E / softness_level
SAFE = 2.0**90
HI = lax.Precision.HIGHEST
f32 = jnp.float32
bf16 = jnp.bfloat16
VMEM = pl.BlockSpec(memory_space=pltpu.VMEM)


def params():
    return pltpu.CompilerParams(vmem_limit_bytes=24 * 2**20)


def pinned(x):
    return pltpu.with_memory_space_constraint(x, pltpu.VMEM)


def select(chooser, x):
    high = x.astype(bf16)
    rest = x - high.astype(f32)
    mid = rest.astype(bf16)
    low = (rest - mid.astype(f32)).astype(bf16)
    terms = jnp.concatenate([high, mid, low], axis=1)
    out = lax.dot_general(chooser, terms, (((1,), (0,)), ((), ())), preferred_element_type=f32)
    n = x.shape[1]
    return out[:, :n] + out[:, n : 2 * n] + out[:, 2 * n :]


def eye():
    return lax.broadcasted_iota(jnp.int32, (128, 128), 0) == lax.broadcasted_iota(
        jnp.int32, (128, 128), 1
    )


def spread_kernel(list_ref, x_ref, out_ref, held, note, sems):
    devices, units = out_ref.shape[0], out_ref.shape[1]
    own = units - 1
    parts = sems.shape[0]
    copies = []
    for part in range(parts):
        rows = pl.ds(part * own // parts * devices, own // parts * devices)
        copies.append(pltpu.make_async_copy(x_ref.at[rows], held.at[rows], sems.at[part]))
        copies[-1].start()
    wanted = list_ref[...]
    owner = ((wanted.astype(f32) + 0.5) * (1.0 / own)).astype(jnp.int32)
    place = wanted - owner * own
    row = lax.broadcasted_iota(jnp.int32, (2, BLOCK), 0)
    note[...] = jnp.where(
        row == 0, jnp.broadcast_to(owner, (2, BLOCK)), jnp.broadcast_to(place, (2, BLOCK))
    ).astype(f32).astype(bf16)
    for part in range(parts):
        copies[part].wait()

        def one(p, _):
            for block in range(part * own // parts, (part + 1) * own // parts):
                out_ref[p, block] = held[block * devices + p]
            if part == 0:
                out_ref[p, own] = note[...]
            return 0

        lax.fori_loop(0, devices, one, 0)


def spread_call(wanted, pairs, devices):
    units = pairs.shape[0] // devices + 1
    return pl.pallas_call(
        spread_kernel,
        out_shape=jax.ShapeDtypeStruct((devices, units) + pairs.shape[1:], pairs.dtype),
        in_specs=[VMEM, pl.BlockSpec(memory_space=pltpu.HBM)],
        out_specs=VMEM,
        scratch_shapes=[
            pltpu.VMEM(pairs.shape, pairs.dtype),
            pltpu.VMEM(pairs.shape[1:], pairs.dtype),
            pltpu.SemaphoreType.DMA((4,)),
        ],
        compiler_params=params(),
    )(wanted, pltpu.with_memory_space_constraint(pairs, pltpu.HBM))


def gather_kernel(own, size, table_ref, out_ref, lists_ref, tail, index, scalars, sem):
    owners = lists_ref.shape[0]
    for i in range(owners):
        tail[i] = table_ref[i * (own + 1) + own]
    pairs = tail[...].astype(f32)
    lists_ref[...] = (pairs[:, 0, :] * float(own) + pairs[:, 1, :]).astype(jnp.int32)
    index[...] = (pairs[:, 0, :] * float(own + 1) + pairs[:, 1, :]).astype(jnp.int32)
    copy = pltpu.make_async_copy(index, scalars, sem)
    copy.start()
    copy.wait()

    def one(i, _):
        for k in range(size):
            out_ref[i * size + k] = table_ref[scalars[i, k]]
        return 0

    lax.fori_loop(0, owners, one, 0)


def gather_call(table, owners, size):
    own = table.shape[0] // owners - 1
    width = table.shape[2]
    return pl.pallas_call(
        functools.partial(gather_kernel, own, size),
        out_shape=[
            jax.ShapeDtypeStruct((owners * size,) + table.shape[1:], table.dtype),
            jax.ShapeDtypeStruct((owners, width), jnp.int32),
        ],
        in_specs=[VMEM],
        out_specs=[VMEM] * 2,
        scratch_shapes=[
            pltpu.VMEM((owners,) + table.shape[1:], table.dtype),
            pltpu.VMEM((owners, width), jnp.int32),
            pltpu.SMEM((owners, width), jnp.int32),
            pltpu.SemaphoreType.DMA,
        ],
        compiler_params=params(),
    )(table)


def finish_score(v_ref, lse_ref, pace, sums, tops, highest):
    rows = v_ref.shape[0]
    chunks = rows // 128
    lse_ref[0:chunks, :] = jnp.zeros((chunks, 128), f32)

    @pl.when(jnp.logical_not(highest < SAFE))
    def _():
        lane = lax.broadcasted_iota(jnp.int32, (8, 128), 1)

        def body(step, _):
            at = pl.ds(pl.multiple_of(step * 8, 8), 8)
            t = v_ref[at, :] * pace[...]
            m = jnp.max(t, axis=1, keepdims=True)
            total = jnp.sum(jnp.exp2(t - m), axis=1, keepdims=True)
            tops[at, :] = jnp.broadcast_to(m, (8, 128))
            sums[at, :] = jnp.where(lane == 0, total, 0.0)
            return 0

        lax.fori_loop(0, rows // 8, body, 0)
        for c in range(chunks):
            lse_ref[c : c + 1, :] = jnp.sum(
                jnp.where(eye(), tops[c * 128 : (c + 1) * 128, :], 0.0), axis=0, keepdims=True
            )

    total = lax.dot_general(
        jnp.ones((8, 128), f32), sums[...], (((1,), (1,)), ((), ())), precision=HI, preferred_element_type=f32
    )
    logs = LOG2E * jnp.log(total)
    for c in range(chunks):
        lse_ref[c : c + 1, :] += logs[0:1, c * 128 : (c + 1) * 128]


def values_kernel(blocks, x_ref, y_ref, v_ref, lse_ref, wide, yt, pace, sums, tops):
    half = BLOCK // 2
    wide[...] = y_ref[...].astype(f32)
    for k in range(blocks):
        for side in range(2):
            at = k * BLOCK + side * half
            yt[at : at + half, :] = wide[pl.ds(2 * k + side, half, stride=2 * blocks), :].astype(bf16)
    tile_c = 1024
    tiles = v_ref.shape[1] // tile_c
    sums[...] = jnp.zeros(sums.shape, f32)

    def product(step):
        cols = pl.ds(pl.multiple_of(step * tile_c, tile_c), tile_c)
        return cols, lax.dot_general(
            x_ref[...], yt[cols, :], (((1,), (1,)), ((), ())), preferred_element_type=f32
        )

    def tile(step, _):
        cols, s = product(step)
        grown = 1.0 + jnp.exp2(s * LOG2E)
        v_ref[:, cols] = jnp.log(grown)
        e = grown * grown
        part = e[:, 0:128]
        for k in range(1, tile_c // 128):
            part = part + e[:, k * 128 : (k + 1) * 128]
        sums[...] += part
        return 0

    lax.fori_loop(0, tiles, tile, 0)
    highest = jnp.max(sums[...])

    @pl.when(jnp.logical_not(highest < SAFE))
    def _():
        def again(step, _):
            cols, s = product(step)
            v_ref[:, cols] = jnp.maximum(s, 0.0) + jnp.log(1.0 + jnp.exp2(jnp.abs(s) * -LOG2E))
            return 0

        lax.fori_loop(0, tiles, again, 0)
        pace[...] = jnp.full(pace.shape, SCALE, f32)

    finish_score(v_ref, lse_ref, pace, sums, tops, highest)


def score_scratch(rows, width):
    return [pltpu.VMEM((8, width), f32), pltpu.VMEM((rows, 128), f32), pltpu.VMEM((rows, 128), f32)]


def values_call(x, y, blocks):
    rows, width = x.shape[0], blocks * BLOCK
    return pl.pallas_call(
        functools.partial(values_kernel, blocks),
        out_shape=[
            pltpu.VMEM((rows, width), f32),
            jax.ShapeDtypeStruct((rows // 128, 128), f32),
        ],
        in_specs=[VMEM] * 2,
        out_specs=[VMEM] * 2,
        scratch_shapes=[pltpu.VMEM(y.shape, f32), pltpu.VMEM(y.shape, bf16)] + score_scratch(rows, width),
        compiler_params=params(),
    )(x, y)


def score(v_ref, lse_ref, pace, sums, tops):
    rows, width = v_ref.shape
    step_rows = 128

    def body(step, highest):
        base = pl.multiple_of(step * step_rows, step_rows)
        total = [None] * (step_rows // 8)
        for k in range(width // 128):
            cols = slice(k * 128, (k + 1) * 128)
            scale = pace[:, cols]
            for part in range(step_rows // 8):
                e = jnp.exp2(v_ref[pl.ds(base + part * 8, 8), cols] * scale)
                total[part] = e if k == 0 else total[part] + e
        for part in range(step_rows // 8):
            sums[pl.ds(base + part * 8, 8), :] = total[part]
            highest = jnp.maximum(highest, total[part])
        return highest

    highest = lax.fori_loop(0, rows // step_rows, body, jnp.zeros((8, 128), f32))
    finish_score(v_ref, lse_ref, pace, sums, tops, jnp.max(highest))


def pace_step(pace, util, limit):
    return jnp.sqrt(pace * jnp.minimum(limit / jnp.maximum(util, util_floor), pacing_cap))


def spread_pace(p, pace):
    for k in range(p.shape[0]):
        pace[:, k * BLOCK : (k + 1) * BLOCK] = jnp.broadcast_to(p[k : k + 1, :] * SCALE, (8, BLOCK))


def received(pick_ref, near_ref, mate_ref):
    both = [ref[...].reshape(-1, BLOCK) for ref in (near_ref, mate_ref)]
    return select(pick_ref[...], jnp.concatenate(both, axis=0))


def second_score_kernel(
    flag_slot, util_ref, near_ref, mate_ref, pick_ref, v_in, v_ref, lse_ref, p_ref, limit_ref, pace, sums, tops
):
    blocks = util_ref.shape[0]
    got = received(pick_ref, near_ref, mate_ref)
    limit = got[blocks:, :]
    p = pace_step(jnp.ones(limit.shape, f32), util_ref[...] + got[:blocks, :], limit)
    p_ref[...] = p
    limit_ref[...] = limit
    spread_pace(p, pace)
    score(v_in, lse_ref, pace, sums, tops)
    flag = jnp.zeros((8, BLOCK), f32)
    for ref in (near_ref, mate_ref):
        for chip in range(ref.shape[0]):
            flag = jnp.maximum(flag, ref[chip, flag_slot : flag_slot + 1, :])
    lse_ref[v_in.shape[0] // 128 :, :] = flag


def score_kernel(
    util_ref, near_ref, mate_ref, pick_ref, limit_ref, old_ref, v_in, v_ref, lse_ref, p_ref, pace, sums, tops
):
    util = util_ref[...] + received(pick_ref, near_ref, mate_ref)
    p = pace_step(old_ref[...], util, limit_ref[...])
    p_ref[...] = p
    spread_pace(p, pace)
    score(v_in, lse_ref, pace, sums, tops)


def score_call(kernel, v, args, lse_rows, outs):
    rows, width = v.shape
    small = jax.ShapeDtypeStruct((width // BLOCK, BLOCK), f32)
    return pl.pallas_call(
        kernel,
        out_shape=[pltpu.VMEM((rows, width), f32), jax.ShapeDtypeStruct((lse_rows, 128), f32)]
        + [small] * outs,
        in_specs=[VMEM] * (len(args) + 1),
        out_specs=[VMEM] * (2 + outs),
        scratch_shapes=score_scratch(rows, width),
        input_output_aliases={len(args): 0},
        compiler_params=params(),
    )(*args, pinned(v))


def combine(lse_refs, chunks):
    parts = [ref[0:chunks, :] for ref in lse_refs]
    top = functools.reduce(jnp.maximum, parts)
    return top + LOG2E * jnp.log(sum(jnp.exp2(part - top) for part in parts))


def utility(lse, v_ref, util_ref, pace, column):
    rows, width = v_ref.shape
    for c in range(rows // 128):
        column[c * 128 : (c + 1) * 128, :] = jnp.transpose(jnp.broadcast_to(lse[c : c + 1, :], (128, 128)))
    blocks = width // BLOCK
    step_rows = 128

    def body(step, _):
        base = pl.multiple_of(step * step_rows, step_rows)
        for k in range(blocks):
            cols = slice(k * BLOCK, (k + 1) * BLOCK)
            scale = pace[:, cols]
            acc = None
            for part in range(step_rows // 8):
                at = pl.ds(base + part * 8, 8)
                v = v_ref[at, cols]
                term = jnp.exp2(v * scale - column[at, :]) * v
                acc = term if acc is None else acc + term
            util_ref[k : k + 1, :] += jnp.sum(acc, axis=0, keepdims=True)
        return 0

    util_ref[0:blocks, :] = jnp.zeros((blocks, BLOCK), f32)
    lax.fori_loop(0, rows // step_rows, body, 0)


def utility_kernel(columns, first, *refs):
    lse_refs, refs = refs[:columns], refs[columns:]
    if first:
        put_ref, own_put_ref, limit_ref, v_in, v_ref, util_ref, send_ref, pace, column = refs
        pace[...] = jnp.full(pace.shape, SCALE, f32)
    else:
        put_ref, p_ref, v_in, v_ref, util_ref, send_ref, pace, column = refs
        spread_pace(p_ref[...], pace)
    utility(combine(lse_refs, v_in.shape[0] // 128), v_in, util_ref, pace, column)
    send = select(put_ref[...], util_ref[...])
    if first:
        send = send + select(own_put_ref[...], limit_ref[...])
    send_ref[...] = send.reshape(send_ref.shape)


def last_utility_kernel(columns, *refs):
    lse_refs, refs = refs[:columns], refs[columns:]
    put_ref, p_ref, v_in, v_ref, both_ref, send_ref, price_ref, pace, column = refs
    lse = combine(lse_refs, v_in.shape[0] // 128)
    price_ref[...] = lse * (softness_level * LN2)
    blocks = p_ref.shape[0]
    spread_pace(p_ref[...], pace)
    utility(lse, v_in, both_ref, pace, column)
    both_ref[blocks:, :] = p_ref[...]
    send_ref[...] = select(put_ref[...], both_ref[...]).reshape(send_ref.shape)


def utility_call(kernel, v, args, util_rows, send_shape, price):
    rows, width = v.shape
    outs = [
        pltpu.VMEM((rows, width), f32),
        jax.ShapeDtypeStruct((util_rows, BLOCK), f32),
        jax.ShapeDtypeStruct(send_shape, f32),
    ]
    if price:
        outs.append(jax.ShapeDtypeStruct((rows // 128, 128), f32))
    return pl.pallas_call(
        kernel,
        out_shape=outs,
        in_specs=[VMEM] * (len(args) + 1),
        out_specs=[VMEM] * len(outs),
        scratch_shapes=[pltpu.VMEM((8, width), f32), pltpu.VMEM((rows, 128), f32)],
        input_output_aliases={len(args): 0},
        compiler_params=params(),
    )(*args, pinned(v))


def last_pace_kernel(recv_ref, back_ref, limit_ref, out_ref):
    limit = limit_ref[...]
    own = limit.shape[0]
    back = back_ref[...]
    got = select(back, recv_ref[...].reshape(-1, BLOCK))
    count = jnp.sum(back[own:, :].astype(f32), axis=1, keepdims=True)
    lone = jnp.ones(limit.shape, f32)
    for _ in range(ROUNDS - 1):
        lone = pace_step(lone, jnp.zeros(limit.shape, f32), limit)
    pace = jnp.where(count > 0.0, got[own:, :] / jnp.maximum(count, 1.0), lone)
    out = pace_step(pace, got[:own, :], limit)
    row = lax.broadcasted_iota(jnp.int32, (BLOCK, BLOCK), 0)
    column = lax.broadcasted_iota(jnp.int32, (BLOCK, BLOCK), 1)
    half = BLOCK // 2
    home = jnp.where(row < half, 2 * row, 2 * (row - half) + 1)
    out_ref[...] = jnp.transpose(select((home == column).astype(f32).T.astype(bf16), jnp.transpose(out)))


def before(flags, axis):
    size = flags.shape[axis]
    order = jnp.arange(size)
    less = (order[:, None] < order[None, :]).astype(f32)
    moved = jnp.moveaxis(flags, axis, -1).astype(f32)
    return jnp.moveaxis(jnp.dot(moved, less), -1, axis).astype(jnp.int32)


def swap(x, axis):
    return lax.all_to_all(x, axis, split_axis=0, concat_axis=0, tiled=True)


def slots_of(shared):
    first = shared + 2 * CAP + 1
    return shared, -(-first // 8) * 8


def share_plan(lists, me, equal, placed, back, limits, shared):
    owners, size = lists.shape
    chips = owners // 2
    core = me % 2
    mate = me + 1 - 2 * core
    slots, first_slots = slots_of(shared)
    peer = jnp.arange(owners, dtype=jnp.int32)
    mate_list = lax.dynamic_index_in_dim(lists, mate, 0, keepdims=False)
    mate_equal = (lists[:, :, None] == mate_list[None, None, :]) & (peer != mate)[:, None, None]
    gives = jnp.any(equal, axis=1).reshape(chips, 2, size).any(axis=1)
    takes = jnp.any(equal, axis=2) | jnp.any(mate_equal, axis=2)
    slot = jnp.arange(shared, dtype=jnp.int32)[None, :, None]
    put = ((before(gives, 1)[:, None, :] == slot) & gives[:, None, :]).astype(f32)
    take_slot = ((before(takes, 1)[:, None, :] == slot) & takes[:, None, :]).astype(f32)
    pick = jnp.einsum("isk,ikw->isw", take_slot, equal.astype(f32))
    crowded = jnp.any(jnp.sum(gives.astype(jnp.int32), axis=1) > shared)

    def grow(x, low, total):
        return jnp.pad(x, ((0, 0), (low, total - low - x.shape[1]), (0, 0)))

    def sides(x):
        x = x.reshape(chips, 2, x.shape[1], size)
        x = jnp.where(core == 0, x, x[:, ::-1])
        return x.transpose(3, 1, 0, 2).reshape(size, -1).astype(bf16)

    none = jnp.zeros_like(placed)
    for_me = jnp.where(core == 0, jnp.concatenate([placed, none], 1), jnp.concatenate([none, placed], 1))
    first_pick = jnp.concatenate(
        [sides(grow(pick, 0, first_slots)), sides(grow(for_me, shared, first_slots))], axis=0
    )
    own_blocks = back.shape[2]
    own_put = grow(back.reshape(chips, 2 * CAP, own_blocks), shared, first_slots)
    mark = (jnp.arange(first_slots) == shared + 2 * CAP).astype(f32)[None, :, None]
    own_put = jnp.concatenate([own_put, jnp.broadcast_to(mark, (chips, first_slots, 1))], axis=2)
    return (
        put.reshape(chips * slots, size).astype(bf16),
        sides(pick),
        grow(put, 0, first_slots).reshape(chips * first_slots, size).astype(bf16),
        own_put.reshape(chips * first_slots, own_blocks + 1).astype(bf16),
        first_pick,
        jnp.concatenate([limits, jnp.broadcast_to(crowded.astype(f32), (1, BLOCK))], axis=0),
    )


def rounds(columns, shared, imp_vectors, mine, limits, plan, last_put, last_back):
    put, pick, first_put, own_put, first_pick, known = plan
    size = put.shape[1]
    slots, first_slots = slots_of(shared)
    chips = put.shape[0] // slots
    owners = 2 * chips
    chunks = imp_vectors.shape[0] // 128

    def exchange(send):
        groups = [[2 * chip + core for chip in range(chips)] for core in range(2)]
        near = lax.all_to_all(
            send, "imp", split_axis=0, concat_axis=0, tiled=True, axis_index_groups=groups
        )
        return [near, lax.ppermute(near, "imp", [(i, i ^ 1) for i in range(owners)])]

    def everywhere(lse):
        shifts = sorted(range(1, columns), key=lambda d: -min(d, columns - d))
        return [lse] + [
            lax.ppermute(lse, "ad", [(i, (i + d) % columns) for i in range(columns)]) for d in shifts
        ]

    v, lse = values_call(imp_vectors, mine, size)
    v, util, send = utility_call(
        functools.partial(utility_kernel, columns, True),
        v, everywhere(lse) + [first_put, own_put, known], size, (chips, first_slots, BLOCK), False,
    )
    v, lse, pace, wanted_limits = score_call(
        functools.partial(second_score_kernel, shared + 2 * CAP),
        v, [util] + exchange(send) + [first_pick], chunks + 8, 2,
    )
    every = everywhere(lse)
    flags = every
    for step in range(2, ROUNDS):
        v, util, send = utility_call(
            functools.partial(utility_kernel, columns, False),
            v, every + [put, pace], size, (chips, slots, BLOCK), False,
        )
        v, lse, pace = score_call(
            score_kernel, v, [util] + exchange(send) + [pick, wanted_limits, pace], chunks, 1
        )
        every = everywhere(lse)
    _, _, send, prices = utility_call(
        functools.partial(last_utility_kernel, columns),
        v, every + [last_put, pace], 2 * size, (owners, 2 * CAP, BLOCK), True,
    )
    send, flags = lax.optimization_barrier((send, flags))
    recv = swap(send, "imp")
    final = pl.pallas_call(
        last_pace_kernel,
        out_shape=jax.ShapeDtypeStruct(limits.shape, f32),
        in_specs=[VMEM] * 3,
        out_specs=VMEM,
        compiler_params=params(),
    )(recv, last_back, limits)
    over = functools.reduce(jnp.maximum, [part[chunks, 0] for part in flags])
    return final, prices, over


def per_device(imp_vectors, ad_vectors, spend_limits, targets):
    owners = lax.axis_size("imp")
    columns = lax.axis_size("ad")
    me = lax.axis_index("imp")
    emb = imp_vectors.shape[1]
    own_blocks = ad_vectors.shape[0] // BLOCK
    wanted = targets.reshape(-1)
    size = wanted.shape[0]
    half = BLOCK // 2
    limits = spend_limits.reshape(own_blocks, half, 2).transpose(0, 2, 1).reshape(own_blocks, BLOCK)

    owner_of = wanted // own_blocks
    wide_list = jnp.pad(wanted[None, :], ((0, 0), (0, emb - size)))
    pieces = spread_call(wide_list, ad_vectors.reshape(own_blocks * half, 2, emb), half)
    table = swap(pieces, "imp").reshape(owners * (own_blocks + 1), 2, emb)
    chosen, lists = gather_call(table, owners, size)
    lists = lists[:, :size]
    mine = swap(chosen.reshape(owners, size, 2, emb), "imp").reshape(owners * size * 2, emb)

    peer = jnp.arange(owners, dtype=jnp.int32)
    equal = (lists[:, :, None] == wanted[None, None, :]) & (peer != me)[:, None, None]
    rank_of = jnp.sum(
        (owner_of[:, None] == owner_of[None, :]) & (jnp.arange(size)[None, :] < jnp.arange(size)[:, None]),
        axis=1,
    )
    lane = jnp.arange(CAP, dtype=jnp.int32)
    placed = (
        (owner_of[None, None, :] == peer[:, None, None]) & (rank_of[None, None, :] == lane[None, :, None])
    ).astype(f32)
    at_me = lists // own_blocks == me
    asked = (before(at_me, 1)[:, None, :] == lane[None, :, None]) & at_me[:, None, :]
    local = jnp.arange(own_blocks, dtype=jnp.int32)
    here = (lists[:, :, None] - me * own_blocks) == local[None, None, :]
    back = jnp.einsum("irk,ikl->irl", asked.astype(f32), here.astype(f32))

    def doubled(x):
        none = jnp.zeros_like(x)
        both = jnp.concatenate(
            [jnp.concatenate([x, none], axis=2), jnp.concatenate([none, x], axis=2)], axis=1
        )
        return both.reshape(owners * 2 * CAP, 2 * x.shape[2]).astype(bf16)

    last_put, last_back = doubled(placed), doubled(back).T
    narrow = share_plan(lists, me, equal, placed, back, limits, SHARED)
    ready = (mine, narrow, last_put, last_back, limits)
    ready = jax.tree.map(lambda x: with_layout_constraint(x, Layout(tuple(range(x.ndim)))), ready)
    mine, narrow, last_put, last_back, limits = lax.optimization_barrier(ready)

    final, prices, over = rounds(columns, SHARED, imp_vectors, mine, limits, narrow, last_put, last_back)

    def take_wide():
        plan = share_plan(lists, me, equal, placed, back, limits, size)
        return rounds(columns, size, imp_vectors, mine, limits, plan, last_put, last_back)[:2]

    final, prices = lax.cond(over > 0.5, take_wide, lambda: (final, prices))
    return final.reshape(-1), prices.reshape(-1)


def solution(mesh):
    return jax.shard_map(
        per_device,
        mesh=mesh,
        in_specs=(P("imp", None), P(("imp", "ad"), None), P(("imp", "ad")), P("imp", "ad", None)),
        out_specs=(P(("imp", "ad")), P("imp")),
        check_vma=False,
    )
```
